512 devices in a mesh: seq: 64 (over y, z), head: 8 (over x, core).
Axes of the slice: x: 4, y: 4, z: 16, core: 2. Of those that a mesh axis runs over, the one named last changes fastest.
Arguments:
- queries: bfloat16 [32768, 16, 128], P('seq', 'head'), may hold values from -5 to 5
- keys: bfloat16 [32768, 16, 128], P('seq', 'head'), may hold values from -5 to 5
- values: bfloat16 [32768, 16, 128], P('seq', 'head'), may hold values from -6 to 6
- layer_grad: bfloat16 [32768, 2048], P('seq', 'head'), may hold values from -6 to 6
- out_proj: bfloat16 [16, 128, 2048], P('head'), may hold values from -0.125 to 0.125
- cluster: int32 [16, 32768], P('head', 'seq'), may hold values from 0 to 511, as said below
- slot: int32 [16, 32768], P('head', 'seq'), may hold values from 0 to 2, as said below
- tile_of: int32 [16, 512], P('head'), may hold values from 0 to 511, as said below
Outputs:
- query_grad: bfloat16 [32768, 16, 128], P('seq', 'head')
- key_grad: bfloat16 [32768, 16, 128], P('seq', 'head')
- value_grad: bfloat16 [32768, 16, 128], P('seq', 'head')
- centroid_sums: float32 [16, 512, 128], P('head', 'seq')
The draws below stay inside these ranges and needn't reach their ends.
Inputs may be any that keep to these rules, and one draw needn't show every extreme that they name: For each head, among the 512 tokens of one device at most 3 are in one cluster, and at most 16 are in clusters whose tile_of values give the same owner (tile // 8); in every head one cluster has exactly 3 tokens on every device, and one owner exactly 16 from every device. `slot`: for each head and each device, the tokens of one cluster carry slots 0, 1, 2, ... in the order of their positions. `tile_of`: for each head a permutation of the clusters.
All inputs are finite; a program needn't handle non-finite values.
Results may differ from the reference program's by a relative error of at most 0.0087.
Values may be sent and summed in bfloat16 or wider, within the bound.
A program may use at most 64 MiB of HBM per device.

```python
import jax
import jax.numpy as jnp
from jax import lax

D = 2048
DH = 128
CL_DEV = 8
TOK_DEV = 512
HEADS = 16
CLUSTERS = 512
TOKENS = 32768
MOST = 3
SEND_CAP = 16
N_SEQ = 64


def routing(key):
    key = jax.random.fold_in(key, 101)
    streams = jax.random.split(key, 6)
    tile_of = jax.vmap(lambda each: jax.random.permutation(each, CLUSTERS))(jax.random.split(streams[0], HEADS)).astype(jnp.int32)
    popular = jax.random.randint(streams[1], (HEADS, 1, CLUSTERS, 1), 0, 1000)
    full_tile = jax.random.randint(streams[2], (HEADS, 1, 1, 1), 0, CLUSTERS)
    increments = jax.random.randint(streams[3], (HEADS, N_SEQ, CLUSTERS, MOST), 1, 200)
    falling = increments[..., :1] - jnp.cumsum(increments, axis=3)
    jitter = jax.random.randint(streams[4], (HEADS, N_SEQ, CLUSTERS, 1), 0, 1000)
    tile_ids = jnp.arange(CLUSTERS, dtype=jnp.int32).reshape(1, 1, CLUSTERS, 1)
    boost_term = jnp.where(tile_ids // CL_DEV == full_tile // CL_DEV, 20000, 0) + jnp.where(tile_ids == full_tile, 40000, 0)
    priority = 30000 + popular + jitter + falling + boost_term
    slot_order = tile_ids * MOST + jnp.arange(MOST, dtype=jnp.int32).reshape(1, 1, 1, MOST)
    priority_key = priority * 16384 + (16383 - slot_order)
    per_owner = priority_key.reshape(HEADS, N_SEQ, N_SEQ, CL_DEV * MOST)
    threshold = lax.top_k(per_owner, SEND_CAP)[0][..., -1:]
    eligible = jnp.where(per_owner >= threshold, per_owner, -1).reshape(HEADS, N_SEQ, CLUSTERS * MOST)
    chosen = jnp.sort(lax.top_k(eligible, TOK_DEV)[1], axis=-1).astype(jnp.int32)
    tile_pick = chosen // MOST
    slot_pick = chosen % MOST
    shuffle = jax.vmap(lambda each: jax.random.permutation(each, TOK_DEV))(jax.random.split(streams[5], HEADS * N_SEQ)).astype(jnp.int32).reshape(HEADS, N_SEQ, TOK_DEV)
    arrangement = jnp.argsort(tile_pick * TOK_DEV + shuffle, axis=-1)
    position = jnp.take_along_axis(shuffle, arrangement, axis=-1)
    head_index = jnp.arange(HEADS, dtype=jnp.int32)[:, None, None]
    block_index = jnp.arange(N_SEQ, dtype=jnp.int32)[None, :, None]
    tile_at = jnp.zeros((HEADS, N_SEQ, TOK_DEV), jnp.int32).at[head_index, block_index, position].set(tile_pick)
    slot_at = jnp.zeros((HEADS, N_SEQ, TOK_DEV), jnp.int32).at[head_index, block_index, position].set(slot_pick)
    inverse = jnp.argsort(tile_of, axis=-1).astype(jnp.int32)
    cluster = jnp.take_along_axis(inverse, tile_at.reshape(HEADS, TOKENS), axis=1)
    return (cluster, slot_at.reshape(HEADS, TOKENS), tile_of)


def row_scales(key, lower, upper):
    return jnp.exp(jax.random.uniform(key, (TOKENS, HEADS, 1), jnp.float32, jnp.log(lower), jnp.log(upper)))


def draw_cluster(key, part):
    return routing(key)[0]


def draw_slot(key, part):
    return routing(key)[1]


def draw_tile_of(key, part):
    return routing(key)[2]


def draw_queries(key, part):
    key = jax.random.fold_in(key, 1)
    key_scale, key_body = jax.random.split(key, 2)
    drawn = jax.random.normal(key_body, (TOKENS, HEADS, DH), jnp.float32) * row_scales(key_scale, 0.6, 2.0)
    return jnp.clip(drawn, -5.0, 5.0).astype(jnp.bfloat16)


def draw_keys(key, part):
    key = jax.random.fold_in(key, 2)
    key_scale, key_body = jax.random.split(key, 2)
    drawn = jax.random.normal(key_body, (TOKENS, HEADS, DH), jnp.float32) * row_scales(key_scale, 0.6, 2.0)
    return jnp.clip(drawn, -5.0, 5.0).astype(jnp.bfloat16)


def shard_levels(own_key, shape, cuts, least, high):
    loudness, own = 1.0, jax.random.fold_in(own_key, 6)
    for dim, shards_of in cuts:
        steps = jnp.exp(jax.random.uniform(jax.random.fold_in(own, dim), (shards_of,), jnp.float32, least / len(cuts), high / len(cuts)))
        loudness = loudness * jnp.repeat(steps, shape[dim] // shards_of).reshape([-1 if axis == dim else 1 for axis in range(len(shape))])
    return loudness


def centred(own_key, shape, spread, limit, cuts=(), kind=jnp.bfloat16):
    entries = spread * jax.random.normal(own_key, shape, jnp.float32)
    if cuts:
        entries = entries * shard_levels(own_key, shape, cuts, -0.22, 0.18)
    return jnp.clip(entries, -limit, limit).astype(kind)


def setup_inputs(seed: int = 0) -> dict:
    arg_keys = jax.random.split(jax.random.key(seed), 9)
    return {
        "queries": draw_queries(jax.random.fold_in(arg_keys[8], 71), 0),
        "keys": draw_keys(jax.random.fold_in(arg_keys[8], 71), 0),
        "values": centred(arg_keys[2], (TOKENS, HEADS, DH), 1.0, 6.0, ((0, 64), (1, 8))),
        "layer_grad": centred(arg_keys[3], (TOKENS, D), 1.0, 6.0, ((0, 64), (1, 8))),
        "out_proj": centred(arg_keys[4], (HEADS, DH, D), D ** -0.5, 0.125, ((0, 8),)),
        "cluster": draw_cluster(jax.random.fold_in(arg_keys[8], 71), 0),
        "slot": draw_slot(jax.random.fold_in(arg_keys[8], 71), 0),
        "tile_of": draw_tile_of(jax.random.fold_in(arg_keys[8], 71), 0),
    }


def tile_grads(query_tile, key_tile, value_tile, grad_tile, used_rows):
    factor = query_tile.shape[-1] ** (-0.5)
    query_wide = query_tile.astype(jnp.float32)
    key_wide = key_tile.astype(jnp.float32)
    value_wide = value_tile.astype(jnp.float32)
    grad_wide = grad_tile.astype(jnp.float32)
    scores = jnp.einsum('brd,bcd->brc', query_wide, key_wide) * factor
    tile_rows = query_tile.shape[1]
    row_index = jnp.arange(tile_rows)[:, None]
    col_index = jnp.arange(tile_rows)[None, :]
    allowed = (col_index <= row_index)[None] & (used_rows[:, :, None] > 0) & (used_rows[:, None, :] > 0)
    row_max = lax.optimization_barrier(jnp.max(jnp.where(allowed, scores, -1e+30), axis=2, keepdims=True))
    weights = jnp.where(allowed, jnp.exp(scores - row_max), 0.0)
    row_total = jnp.where(used_rows > 0, lax.optimization_barrier(jnp.sum(weights, axis=2)), 1.0)
    weights = weights / row_total[:, :, None]
    weights_low = lax.optimization_barrier(weights.astype(jnp.bfloat16)).astype(jnp.float32)
    attended = jnp.einsum('brc,bcd->brd', weights_low, value_wide)
    diag_term = lax.optimization_barrier(jnp.sum(grad_wide * attended, axis=2))
    dprobs = jnp.einsum('brd,bcd->brc', grad_wide, value_wide)
    dscores = lax.optimization_barrier((weights * (dprobs - diag_term[:, :, None])).astype(jnp.bfloat16)).astype(jnp.float32)
    query_grad = (jnp.einsum('brc,bcd->brd', dscores, key_wide) * factor).astype(jnp.bfloat16)
    key_grad = (jnp.einsum('brc,brd->bcd', dscores, query_wide) * factor).astype(jnp.bfloat16)
    value_grad = jnp.einsum('brc,brd->bcd', weights_low, grad_wide).astype(jnp.bfloat16)
    unit_query = query_wide * lax.rsqrt(lax.optimization_barrier(jnp.sum(query_wide * query_wide, axis=2, keepdims=True)) + 1e-06)
    unit_key = key_wide * lax.rsqrt(lax.optimization_barrier(jnp.sum(key_wide * key_wide, axis=2, keepdims=True)) + 1e-06)
    centroid = jnp.einsum('br,brd->bd', used_rows, unit_query + unit_key)
    return (query_grad, key_grad, value_grad, centroid)

def reference(queries, keys, values, layer_grad, out_proj, cluster, slot, tile_of):
    out_grad = jnp.einsum('tm,hdm->thd', layer_grad.astype(jnp.float32), out_proj.astype(jnp.float32)).astype(jnp.bfloat16)
    capacity = N_SEQ * MOST
    source = jnp.arange(TOKENS, dtype=jnp.int32) // TOK_DEV

    def one_head(inputs):
        query_rows, key_rows, value_rows, grad_rows, cluster_row, slot_row, tile_table = inputs
        tile_index = jnp.take(tile_table, cluster_row).astype(jnp.int32)
        buffer_row = (tile_index * capacity + source * MOST + slot_row).astype(jnp.int32)
        payload = jnp.stack([query_rows, key_rows, value_rows, grad_rows], axis=1)
        tiled = jnp.zeros((CLUSTERS * capacity, 4, DH), payload.dtype).at[buffer_row].set(payload)
        used = jnp.zeros((CLUSTERS * capacity,), jnp.float32).at[buffer_row].set(1.0)
        tiled = tiled.reshape(N_SEQ, CL_DEV, capacity, 4, DH)
        used = used.reshape(N_SEQ, CL_DEV, capacity)

        def tile_group(group):
            block, used_block = group
            query_grad, key_grad, value_grad, centroid = tile_grads(block[:, :, 0], block[:, :, 1], block[:, :, 2], block[:, :, 3], used_block)
            return (jnp.stack([query_grad, key_grad, value_grad], axis=2), centroid)
        gradients, centroid = lax.map(tile_group, (tiled, used))
        gradients = gradients.reshape(CLUSTERS * capacity, 3, DH)[buffer_row]
        return (gradients, centroid.reshape(CLUSTERS, DH))
    gradients, centroid_sums = lax.map(one_head, (jnp.transpose(queries, (1, 0, 2)), jnp.transpose(keys, (1, 0, 2)), jnp.transpose(values, (1, 0, 2)), jnp.transpose(out_grad, (1, 0, 2)), cluster, slot, tile_of))
    gradients = jnp.transpose(gradients, (1, 0, 2, 3))
    return (gradients[:, :, 0], gradients[:, :, 1], gradients[:, :, 2], centroid_sums)
```

```python
import functools

import jax
import jax.numpy as jnp
from jax import lax
from jax.experimental import pallas as pl
from jax.experimental.pallas import tpu as pltpu
from jax.sharding import PartitionSpec as P

MESH = pl.DeviceIdType.MESH
CAP = 16
Z = 16
F32 = jnp.float32
BF16 = jnp.bfloat16
UNUSED = 1 << 20


def iota(shape, dim):
    return lax.broadcasted_iota(jnp.int32, shape, dim)


def one_hot(mask):
    return jnp.where(mask, 1.0, 0.0).astype(BF16)


def matmul(a, b):
    return jnp.dot(a, b, preferred_element_type=F32)


def matmul_nt(a, b):
    return lax.dot_general(a, b, (((1,), (1,)), ((), ())), preferred_element_type=F32)


def matmul_tn(a, b):
    return lax.dot_general(a, b, (((0,), (0,)), ((), ())), preferred_element_type=F32)


def kernel(
    n_seq,
    n_head,
    queries,
    keys,
    values,
    layer_grad,
    out_proj,
    cluster,
    slot,
    tile_of,
    query_grad,
    key_grad,
    value_grad,
    centroid,
    gathered,
    grads_out,
    pack,
    unpack,
    qkv_send,
    qkv_recv,
    og_send,
    og_recv,
    meta_send,
    meta_recv,
    ret_send,
    ret_recv,
    key_sum,
    value_sum,
    gather_send_sem,
    gather_recv_sem,
    qkv_send_sem,
    qkv_recv_sem,
    og_send_sem,
    og_recv_sem,
    meta_send_sem,
    meta_recv_sem,
    ret_send_sem,
    ret_recv_sem,
):
    me = lax.axis_index("seq")
    my_head = lax.axis_index("head")
    me_y, me_z = me // Z, me % Z
    n_y = n_seq // Z
    heads, tokens = cluster.shape
    clusters = tile_of.shape[1]
    size = queries.shape[1] // heads
    rows = n_seq * CAP
    columns = layer_grad.shape[1]

    def ahead(k):
        return {"seq": lax.rem(me_y + k // Z, n_y) * Z + lax.rem(me_z + k % Z, Z)}

    def behind(k):
        return {"seq": lax.rem(me_y + n_y - k // Z, n_y) * Z + lax.rem(me_z + Z - k % Z, Z)}

    def peer(j):
        return {"head": lax.rem(my_head + j, n_head)}

    barrier = pltpu.get_barrier_semaphore()

    @pl.loop(1, n_seq)
    def _(k):
        pl.semaphore_signal(barrier, inc=1, device_id=ahead(k), device_id_type=MESH)

    @pl.loop(1, n_head)
    def _(j):
        pl.semaphore_signal(barrier, inc=1, device_id=peer(j), device_id_type=MESH)

    def send(src, dst, send_sem, recv_sem, target):
        pltpu.make_async_remote_copy(
            src_ref=src,
            dst_ref=dst,
            send_sem=send_sem,
            recv_sem=recv_sem,
            device_id=target,
            device_id_type=MESH,
        ).start()

    def send_all(src, dst, send_sem, recv_sem, target):
        @pl.loop(1, n_seq)
        def _(k):
            send(src.at[k], dst.at[k], send_sem, recv_sem, target(k))

    def wait_all(buffer, sem, count):
        part = buffer.at[pl.ds(1, count - 1)]
        pltpu.make_async_copy(part, part, sem).wait()

    earlier = one_hot(iota((tokens, tokens), 0) < iota((tokens, tokens), 1))
    same = one_hot(iota((tokens, tokens), 0) == iota((tokens, tokens), 1))
    meta = jnp.zeros((n_seq, 128), F32)
    for h in range(heads):
        ids = cluster[pl.ds(h, 1), :]
        table = jnp.broadcast_to(tile_of[pl.ds(h, 1), :], (8, clusters))
        table = jnp.where(iota((8, clusters), 0) == 0, table >> 3, table & 7)
        chosen = one_hot(iota((clusters, tokens), 0) == ids)
        found = matmul(table.astype(F32).astype(BF16), chosen).astype(jnp.int32)
        owner, local = found[0:1], found[1:2]
        block = (((owner >> 4) - me_y + n_y) & (n_y - 1)) * Z + (((owner & 15) - me_z + Z) & (Z - 1))
        in_block = iota((n_seq, tokens), 0) == block
        before = matmul(one_hot(in_block), earlier)
        place = jnp.sum(jnp.where(in_block, before, 0.0), axis=0, keepdims=True)
        place_int = place.astype(jnp.int32)
        label = (local * 4 + slot[pl.ds(h, 1), :] + 1).astype(F32)
        labelled = jnp.where(iota((128, tokens), 0) == place_int + CAP * h, label, 0.0).astype(BF16)
        meta += matmul_nt(one_hot(in_block), labelled)
        target = block * CAP + place_int
        pack[h] = one_hot(iota((rows, tokens), 0) == target)
        both = jnp.where(
            iota((8, tokens), 0) == 0, block.astype(F32), jnp.broadcast_to(place, (8, tokens))
        ).astype(BF16)
        both = matmul_nt(same, both).astype(jnp.int32)
        unpack[h] = one_hot(iota((tokens, rows), 1) == both[:, 0:1] * CAP + both[:, 1:2])
    meta_send[...] = meta.reshape(n_seq, 1, 128)

    def pack_part(dst, h, cuts):
        for first in range(0, rows, 256):
            part = pack[h, pl.ds(first, 256), :]
            for i, source in enumerate(cuts):
                moved = matmul(part, source[:, pl.ds(h * size, size)]).astype(BF16)
                dst[h, pl.ds(first // CAP, 256 // CAP), :, pl.ds(i * size, size)] = moved.reshape(
                    256 // CAP, CAP, size
                )

    pack_part(qkv_send, 0, (queries, keys, values))
    pl.semaphore_wait(barrier, n_seq - 1 + n_head - 1)

    @pl.loop(1, n_head)
    def _(j):
        send(layer_grad, gathered.at[j], gather_send_sem, gather_recv_sem, peer(j))

    send_all(meta_send, meta_recv, meta_send_sem, meta_recv_sem, ahead)
    send_all(qkv_send.at[0], qkv_recv.at[0], qkv_send_sem.at[0], qkv_recv_sem.at[0], ahead)
    pack_part(qkv_send, 1, (queries, keys, values))
    meta_recv[0] = meta_send[0]
    for h in range(heads):
        qkv_recv[h, 0] = qkv_send[h, 0]

    wait_all(gathered, gather_recv_sem, n_head)
    total = jnp.zeros((tokens, heads * size), F32)
    for j in range(n_head):
        part = layer_grad[...] if j == 0 else gathered[j]
        source = lax.rem(my_head + n_head - j, n_head)
        weight = out_proj[:, pl.ds(pl.multiple_of(source * columns, columns), columns)]
        total += matmul_nt(part, weight)
    grads_out[...] = total.astype(BF16)
    pack_part(og_send, 0, (grads_out,))
    send_all(og_send.at[0], og_recv.at[0], og_send_sem.at[0], og_recv_sem.at[0], ahead)
    for h in range(1, heads):
        send_all(qkv_send.at[h], qkv_recv.at[h], qkv_send_sem.at[h], qkv_recv_sem.at[h], ahead)
        pack_part(og_send, h, (grads_out,))
        send_all(og_send.at[h], og_recv.at[h], og_send_sem.at[h], og_recv_sem.at[h], ahead)
    for h in range(heads):
        og_recv[h, 0] = og_send[h, 0]

    def codes(index, label):
        k = index >> 4
        source = ((me_y - (k >> 4) + n_y) & (n_y - 1)) * Z + ((me_z - (k & 15) + Z) & (Z - 1))
        used = label > 0
        tile = (label - 1) >> 2
        code = tile * 256 + source * 3 + ((label - 1) & 3)
        return used, tile, code

    factor = size ** (-0.5)
    block_rows = 256
    wait_all(meta_recv, meta_recv_sem, n_seq)
    received = meta_recv[...].reshape(n_seq, 128).astype(BF16)
    for h in range(heads):
        lane_of = one_hot(iota((128, rows), 0) == (iota((128, rows), 1) & 15) + CAP * h)
        spread = matmul(received, lane_of)
        own = iota((n_seq, rows), 0) == iota((n_seq, rows), 1) >> 4
        label_row = jnp.sum(jnp.where(own, spread, 0.0), axis=0, keepdims=True).astype(jnp.int32)
        used_row, tile_row, code_row = codes(iota((1, rows), 1), label_row)
        code_row = jnp.where(used_row, code_row, 2 * UNUSED)
        member = one_hot((iota((8, rows), 0) == tile_row) & used_row)

        wait_all(qkv_recv.at[h], qkv_recv_sem.at[h], n_seq)
        wait_all(og_recv.at[h], og_recv_sem.at[h], n_seq)

        key_sum[...] = jnp.zeros_like(key_sum)
        value_sum[...] = jnp.zeros_like(value_sum)
        every_key = qkv_recv[h, :, :, pl.ds(size, size)].reshape(rows, size)
        every_value = qkv_recv[h, :, :, pl.ds(2 * size, size)].reshape(rows, size)

        @pl.loop(0, rows // block_rows)
        def _(b):
            first = pl.multiple_of(b * (block_rows // CAP), block_rows // CAP)
            chunk = pl.ds(first, block_rows // CAP)
            index = iota((block_rows, n_seq), 0) + b * block_rows
            picked = matmul(one_hot(iota((block_rows, n_seq), 1) == index >> 4), received)
            index = iota((block_rows, 128), 0) + b * block_rows
            lane = iota((block_rows, 128), 1) == (index & 15) + CAP * h
            label = jnp.sum(jnp.where(lane, picked, 0.0), axis=1, keepdims=True).astype(jnp.int32)
            used, tile, code = codes(iota((block_rows, 1), 0) + b * block_rows, label)
            low = jnp.where(used, tile * 256, UNUSED)
            code = jnp.where(used, code, -1)
            query = qkv_recv[h, chunk, :, pl.ds(0, size)].reshape(block_rows, size)
            grad = og_recv[h, chunk, :, :].reshape(block_rows, size)
            scores = matmul_nt(query, every_key) * factor
            allowed = (code_row >= low) & (code_row <= code)
            largest = jnp.max(jnp.where(allowed, scores, -1e30), axis=1, keepdims=True)
            weights = jnp.where(allowed, jnp.exp(scores - largest), 0.0)
            whole = jnp.sum(weights, axis=1, keepdims=True)
            probs = weights / jnp.where(used, whole, 1.0)
            probs_low = probs.astype(BF16)
            dprobs = matmul_nt(grad, every_value)
            stat = jnp.sum(probs_low.astype(F32) * dprobs, axis=1, keepdims=True)
            dscores = (probs * (dprobs - stat)).astype(BF16)
            ret_send[h, chunk, :, pl.ds(0, size)] = (
                (matmul(dscores, every_key) * factor)
                .astype(BF16)
                .reshape(block_rows // CAP, CAP, size)
            )
            key_sum[...] += matmul_tn(dscores, query)
            value_sum[...] += matmul_tn(probs_low, grad)

        ret_send[h, :, :, pl.ds(size, size)] = (
            (key_sum[...] * factor).astype(BF16).reshape(n_seq, CAP, size)
        )
        ret_send[h, :, :, pl.ds(2 * size, size)] = (
            value_sum[...].astype(BF16).reshape(n_seq, CAP, size)
        )
        send_all(ret_send.at[h], ret_recv.at[h], ret_send_sem.at[h], ret_recv_sem.at[h], behind)
        ret_recv[h, 0] = ret_send[h, 0]

        unit = jnp.zeros((rows, size), F32)
        for i in range(2):
            wide = qkv_recv[h, :, :, pl.ds(i * size, size)].reshape(rows, size).astype(F32)
            unit += wide * lax.rsqrt(jnp.sum(wide * wide, axis=1, keepdims=True) + 1e-06)
        high = unit.astype(BF16)
        rest = (unit - high.astype(F32)).astype(BF16)
        centroid[pl.ds(h * 8, 8), :] = matmul(member, high) + matmul(member, rest)

    for h in range(heads):
        wait_all(ret_recv.at[h], ret_recv_sem.at[h], n_seq)
        for i, grad_ref in enumerate((query_grad, key_grad, value_grad)):
            returned = ret_recv[h, :, :, pl.ds(i * size, size)].reshape(rows, size)
            grad_ref[:, pl.ds(h * size, size)] = matmul(unpack[h], returned).astype(BF16)

    wait_all(gathered, gather_send_sem, n_head)
    wait_all(meta_send, meta_send_sem, n_seq)
    for h in range(heads):
        wait_all(qkv_send.at[h], qkv_send_sem.at[h], n_seq)
        wait_all(og_send.at[h], og_send_sem.at[h], n_seq)
        wait_all(ret_send.at[h], ret_send_sem.at[h], n_seq)


def on_device(queries, keys, values, layer_grad, out_proj, cluster, slot, tile_of):
    tokens, heads, size = queries.shape
    n_seq, n_head = lax.axis_size("seq"), lax.axis_size("head")
    rows = n_seq * CAP
    flat = (tokens, heads * size)
    vmem = pl.BlockSpec(memory_space=pltpu.VMEM)
    pair = pltpu.SemaphoreType.DMA((heads,))
    query_grad, key_grad, value_grad, centroid = pl.pallas_call(
        functools.partial(kernel, n_seq, n_head),
        out_shape=[jax.ShapeDtypeStruct(flat, BF16)] * 3
        + [jax.ShapeDtypeStruct((heads * 8, size), F32)],
        in_specs=[vmem] * 8,
        out_specs=[vmem] * 4,
        scratch_shapes=[
            pltpu.VMEM((n_head,) + layer_grad.shape, BF16),
            pltpu.VMEM(flat, BF16),
            pltpu.VMEM((heads, rows, tokens), BF16),
            pltpu.VMEM((heads, tokens, rows), BF16),
            pltpu.VMEM((heads, n_seq, CAP, 3 * size), BF16),
            pltpu.VMEM((heads, n_seq, CAP, 3 * size), BF16),
            pltpu.VMEM((heads, n_seq, CAP, size), BF16),
            pltpu.VMEM((heads, n_seq, CAP, size), BF16),
            pltpu.VMEM((n_seq, 1, 128), F32),
            pltpu.VMEM((n_seq, 1, 128), F32),
            pltpu.VMEM((heads, n_seq, CAP, 3 * size), BF16),
            pltpu.VMEM((heads, n_seq, CAP, 3 * size), BF16),
            pltpu.VMEM((rows, size), F32),
            pltpu.VMEM((rows, size), F32),
            pltpu.SemaphoreType.DMA,
            pltpu.SemaphoreType.DMA,
            pair,
            pair,
            pair,
            pair,
            pltpu.SemaphoreType.DMA,
            pltpu.SemaphoreType.DMA,
            pair,
            pair,
        ],
        compiler_params=pltpu.CompilerParams(
            collective_id=0, has_side_effects=True, vmem_limit_bytes=48 << 20
        ),
        name="routed_attention",
    )(
        queries.reshape(flat),
        keys.reshape(flat),
        values.reshape(flat),
        layer_grad,
        out_proj.reshape(heads * size, -1),
        cluster,
        slot,
        tile_of,
    )
    shape = (tokens, heads, size)
    return (
        query_grad.reshape(shape),
        key_grad.reshape(shape),
        value_grad.reshape(shape),
        centroid.reshape(heads, 8, size),
    )


def solution(mesh):
    in_specs = (
        P("seq", "head", None),
        P("seq", "head", None),
        P("seq", "head", None),
        P("seq", "head"),
        P("head", None, None),
        P("head", "seq"),
        P("head", "seq"),
        P("head", None),
    )
    out_specs = (
        P("seq", "head", None),
        P("seq", "head", None),
        P("seq", "head", None),
        P("head", "seq", None),
    )
    return jax.shard_map(
        on_device, mesh=mesh, in_specs=in_specs, out_specs=out_specs, check_vma=False
    )
```

```python
import functools

import jax
import jax.numpy as jnp
from jax import lax
from jax.experimental import pallas as pl
from jax.experimental.pallas import tpu as pltpu
from jax.sharding import PartitionSpec as P

MESH = pl.DeviceIdType.MESH
CAP = 16
Z = 16
F32 = jnp.float32
BF16 = jnp.bfloat16
UNUSED = 1 << 20


def iota(shape, dim):
    return lax.broadcasted_iota(jnp.int32, shape, dim)


def one_hot(mask):
    return jnp.where(mask, 1.0, 0.0).astype(BF16)


def matmul(a, b):
    return jnp.dot(a, b, preferred_element_type=F32)


def matmul_nt(a, b):
    return lax.dot_general(a, b, (((1,), (1,)), ((), ())), preferred_element_type=F32)


def matmul_tn(a, b):
    return lax.dot_general(a, b, (((0,), (0,)), ((), ())), preferred_element_type=F32)


def kernel(
    n_seq,
    n_head,
    *refs,
):
    inputs, outputs, held, results, refs = refs[:8], refs[8:12], refs[12:20], refs[20:24], refs[24:]
    query_grad, key_grad, value_grad, centroid = results
    queries, keys, values, layer_grad, out_proj, cluster, slot, tile_of = held
    (
        gathered,
        grads_out,
        pack,
        unpack,
        rows_send,
        rows_recv,
        meta_send,
        meta_recv,
        ret_send,
        ret_recv,
        key_sum,
        value_sum,
        grads_back,
        gather_send_sem,
        gather_recv_sem,
        meta_send_sem,
        meta_recv_sem,
        send_sem,
        recv_sem,
        held_sem,
        result_sem,
    ) = refs
    me = lax.axis_index("seq")
    my_head = lax.axis_index("head")
    me_y, me_z = me // Z, me % Z
    n_y = n_seq // Z
    heads, tokens = cluster.shape
    clusters = tile_of.shape[1]
    size = queries.shape[2]
    rows = n_seq * CAP
    columns = layer_grad.shape[1]
    others = n_seq - 1

    def ahead(k):
        return {"seq": lax.rem(me_y + k // Z, n_y) * Z + lax.rem(me_z + k % Z, Z)}

    def behind(k):
        return {"seq": lax.rem(me_y + n_y - k // Z, n_y) * Z + lax.rem(me_z + Z - k % Z, Z)}

    def peer(j):
        return {"head": lax.rem(my_head + j, n_head)}

    fetches = [
        pltpu.make_async_copy(source, target, held_sem.at[i])
        for i, (source, target) in enumerate(zip(inputs, held, strict=True))
    ]
    for fetch in fetches[::-1]:
        fetch.start()

    barrier = pltpu.get_barrier_semaphore()

    @pl.loop(1, n_seq)
    def _(k):
        pl.semaphore_signal(barrier, inc=1, device_id=ahead(k), device_id_type=MESH)

    @pl.loop(1, n_head)
    def _(j):
        pl.semaphore_signal(barrier, inc=1, device_id=peer(j), device_id_type=MESH)

    def remote(src, dst, sent, received, target):
        return pltpu.make_async_remote_copy(
            src_ref=src,
            dst_ref=dst,
            send_sem=sent,
            recv_sem=received,
            device_id=target,
            device_id_type=MESH,
        )

    def wait_all(buffer, sem, first, last):
        part = buffer.at[pl.ds(first, last - first)]
        pltpu.make_async_copy(part, part, sem).wait()

    def lanes(ref, h, first, count):
        return ref.at[h, :, :, pl.ds(first * size, count * size)]

    phases = [
        (lanes(rows_send, 0, 0, 3), lanes(rows_recv, 0, 0, 3), ahead, 1, n_seq),
        (lanes(rows_send, 0, 3, 1), lanes(rows_recv, 0, 3, 1), ahead, 1, n_seq),
    ]
    phases += [(rows_send.at[h], rows_recv.at[h], ahead, 1, n_seq) for h in range(1, heads)]
    phases += [
        (ret_send.at[h], ret_recv.at[h], behind, max(1, first), first + n_seq // 2)
        for h in range(heads)
        for first in (0, n_seq // 2)
    ]

    def nth(i):
        return i

    def message(p, i):
        src, dst, target, _, _ = phases[p]
        k = nth(i)
        return remote(src.at[k], dst.at[k], send_sem.at[p], recv_sem.at[p], target(k))

    def issue(p):
        @pl.loop(*phases[p][3:])
        def _(i):
            message(p, i).start()

    def arrived(p):
        _, dst, _, first, last = phases[p]
        wait_all(dst, recv_sem.at[p], first, last)

    places = []

    def route(h):
        ids = cluster[pl.ds(h, 1), :]
        table = jnp.broadcast_to(tile_of[pl.ds(h, 1), :], (8, clusters))
        table = jnp.where(iota((8, clusters), 0) == 0, table >> 3, table & 7)
        chosen = one_hot(iota((clusters, tokens), 0) == ids)
        found = matmul(table.astype(F32).astype(BF16), chosen).astype(jnp.int32)
        owner, local = found[0:1], found[1:2]
        block = (((owner >> 4) - me_y + n_y) & (n_y - 1)) * Z + (((owner & 15) - me_z + Z) & (Z - 1))
        in_block = iota((n_seq, tokens), 0) == block
        earlier = one_hot(iota((tokens, tokens), 0) < iota((tokens, tokens), 1))
        before = matmul(one_hot(in_block), earlier)
        place = jnp.sum(jnp.where(in_block, before, 0.0), axis=0, keepdims=True)
        place_int = place.astype(jnp.int32)
        target = block * CAP + place_int
        places.append((block, place, local))
        pack[h] = one_hot(iota((rows, tokens), 0) == target)

    def labels():
        meta = jnp.zeros((n_seq, 128), F32)
        for h, (block, place, local) in enumerate(places):
            in_block = iota((n_seq, tokens), 0) == block
            label = (local * 4 + slot[pl.ds(h, 1), :] + 1).astype(F32)
            at = iota((128, tokens), 0) == place.astype(jnp.int32) + CAP * h
            meta += matmul_nt(one_hot(in_block), jnp.where(at, label, 0.0).astype(BF16))
        meta_send[...] = meta.reshape(n_seq, 1, 128)

        @pl.loop(1, n_seq)
        def _(k):
            remote(
                meta_send.at[k], meta_recv.at[k], meta_send_sem, meta_recv_sem, ahead(k)
            ).start()

        meta_recv[0] = meta_send[0]

    def route_back(h):
        block, place, _ = places[h]
        same = one_hot(iota((tokens, tokens), 0) == iota((tokens, tokens), 1))
        both = jnp.where(
            iota((8, tokens), 0) == 0, block.astype(F32), jnp.broadcast_to(place, (8, tokens))
        ).astype(BF16)
        both = matmul_nt(same, both).astype(jnp.int32)
        unpack[h] = one_hot(iota((tokens, rows), 1) == both[:, 0:1] * CAP + both[:, 1:2])

    def of_head(ref):
        return lambda h: ref[:, h, :]

    token_rows = [of_head(ref) for ref in (queries, keys, values)]

    def grads_of(h):
        return grads_out[:, pl.ds(h * size, size)]

    def pack_part(h, first_lane, cuts):
        cuts = [cut(h) for cut in cuts]
        for first in range(0, rows, 256):
            part = pack[h, pl.ds(first, 256), :]
            for i, source in enumerate(cuts):
                moved = matmul(part, source).astype(BF16)
                blocks = pl.ds(first // CAP, 256 // CAP)
                moved = moved.reshape(256 // CAP, CAP, size)
                rows_send[h, blocks, :, pl.ds((first_lane + i) * size, size)] = moved

    for fetch in fetches[5:]:
        fetch.wait()
    route(0)
    for fetch in fetches[:5]:
        fetch.wait()
    pack_part(0, 0, token_rows)
    pl.semaphore_wait(barrier, others + n_head - 1)

    @pl.loop(1, n_head)
    def _(j):
        remote(layer_grad, gathered.at[j], gather_send_sem, gather_recv_sem, peer(j)).start()

    issue(0)
    for h in range(1, heads):
        route(h)
    labels()
    for h in range(1, heads):
        pack_part(h, 0, token_rows)

    wait_all(gathered, gather_recv_sem, 1, n_head)
    total = jnp.zeros((tokens, heads * size), F32)
    for j in range(n_head):
        part = layer_grad[...] if j == 0 else gathered[j]
        source = lax.rem(my_head + n_head - j, n_head)
        weight = out_proj[:, pl.ds(pl.multiple_of(source * columns, columns), columns)]
        total += matmul_nt(part, weight)
    grads_out[...] = total.astype(BF16)
    pack_part(0, 3, (grads_of,))
    issue(1)
    for h in range(1, heads):
        pack_part(h, 3, (grads_of,))
    issue(2)
    for h in range(heads):
        rows_recv[h, 0] = rows_send[h, 0]

    def codes(index, label):
        k = index >> 4
        source = ((me_y - (k >> 4) + n_y) & (n_y - 1)) * Z + ((me_z - (k & 15) + Z) & (Z - 1))
        used = label > 0
        tile = (label - 1) >> 2
        code = tile * 256 + source * 3 + ((label - 1) & 3)
        return used, tile, code

    factor = size ** (-0.5)
    block_rows = 256
    turns = rows // block_rows

    def tiles(h):
        received = meta_recv[...].reshape(n_seq, 128).astype(BF16)
        lane_of = one_hot(iota((128, rows), 0) == (iota((128, rows), 1) & 15) + CAP * h)
        spread = matmul(received, lane_of)
        own = iota((n_seq, rows), 0) == iota((n_seq, rows), 1) >> 4
        label_row = jnp.sum(jnp.where(own, spread, 0.0), axis=0, keepdims=True).astype(jnp.int32)
        used_row, tile_row, code_row = codes(iota((1, rows), 1), label_row)
        code_row = jnp.where(used_row, code_row, 2 * UNUSED)
        member = one_hot((iota((8, rows), 0) == tile_row) & used_row)
        key_sum[...] = jnp.zeros_like(key_sum)
        value_sum[...] = jnp.zeros_like(value_sum)
        every_key = rows_recv[h, :, :, pl.ds(size, size)].reshape(rows, size)
        every_value = rows_recv[h, :, :, pl.ds(2 * size, size)].reshape(rows, size)

        @pl.loop(0, turns)
        def _(b):
            start = pl.multiple_of(b * (block_rows // CAP), block_rows // CAP)
            chunk = pl.ds(start, block_rows // CAP)
            index = iota((block_rows, n_seq), 0) + b * block_rows
            picked = matmul(one_hot(iota((block_rows, n_seq), 1) == index >> 4), received)
            index = iota((block_rows, 128), 0) + b * block_rows
            lane = iota((block_rows, 128), 1) == (index & 15) + CAP * h
            label = jnp.sum(jnp.where(lane, picked, 0.0), axis=1, keepdims=True).astype(jnp.int32)
            used, tile, code = codes(iota((block_rows, 1), 0) + b * block_rows, label)
            low = jnp.where(used, tile * 256, UNUSED)
            code = jnp.where(used, code, -1)
            query = rows_recv[h, chunk, :, pl.ds(0, size)].reshape(block_rows, size)
            grad = rows_recv[h, chunk, :, pl.ds(3 * size, size)].reshape(block_rows, size)
            scores = matmul_nt(query, every_key) * factor
            allowed = (code_row >= low) & (code_row <= code)
            largest = jnp.max(jnp.where(allowed, scores, -1e30), axis=1, keepdims=True)
            weights = jnp.where(allowed, jnp.exp(scores - largest), 0.0)
            whole = jnp.sum(weights, axis=1, keepdims=True)
            probs = weights / jnp.where(used, whole, 1.0)
            probs_low = probs.astype(BF16)
            dprobs = matmul_nt(grad, every_value)
            stat = jnp.sum(probs_low.astype(F32) * dprobs, axis=1, keepdims=True)
            dscores = (probs * (dprobs - stat)).astype(BF16)
            ret_send[h, chunk, :, pl.ds(0, size)] = (
                (matmul(dscores, every_key) * factor)
                .astype(BF16)
                .reshape(block_rows // CAP, CAP, size)
            )
            key_sum[...] += matmul_tn(dscores, query)
            value_sum[...] += matmul_tn(probs_low, grad)

        ret_send[h, :, :, pl.ds(size, size)] = (
            (key_sum[...] * factor).astype(BF16).reshape(n_seq, CAP, size)
        )
        ret_send[h, :, :, pl.ds(2 * size, size)] = (
            value_sum[...].astype(BF16).reshape(n_seq, CAP, size)
        )
        ret_recv[h, 0] = ret_send[h, 0]
        return member

    def centroids(h, member):
        unit = jnp.zeros((rows, size), F32)
        for i in range(2):
            wide = rows_recv[h, :, :, pl.ds(i * size, size)].reshape(rows, size).astype(F32)
            unit += wide * lax.rsqrt(jnp.sum(wide * wide, axis=1, keepdims=True) + 1e-06)
        high = unit.astype(BF16)
        rest = (unit - high.astype(F32)).astype(BF16)
        centroid[h] = matmul(member, high) + matmul(member, rest)

    def finish(h, p):
        part = n_seq // 2
        for first in (0, part):
            arrived(p + first // part)
            blocks, columns = pl.ds(first, part), pl.ds(first * CAP, part * CAP)
            returned = ret_recv[h, blocks].reshape(part * CAP, 3 * size)
            moved = matmul(unpack[h, :, columns], returned)
            if first == 0:
                grads_back[...] = moved
            else:
                moved += grads_back[...]
        for i, grad_ref in enumerate((query_grad, key_grad, value_grad)):
            grad_ref[:, h, :] = moved[:, i * size : (i + 1) * size].astype(BF16)

    wait_all(meta_recv, meta_recv_sem, 1, n_seq)
    arrived(0)
    arrived(1)
    member = tiles(0)
    issue(3)
    issue(4)
    centroids(0, member)
    route_back(0)
    arrived(2)
    member = tiles(1)
    issue(5)
    issue(6)
    centroids(1, member)
    route_back(1)
    finish(0, 3)
    finish(1, 5)
    stores = [
        pltpu.make_async_copy(source, target, result_sem.at[i])
        for i, (source, target) in enumerate(zip(results, outputs, strict=True))
    ]
    for store in stores:
        store.start()

    wait_all(gathered, gather_send_sem, 1, n_head)
    wait_all(meta_send, meta_send_sem, 1, n_seq)
    for p, (src, _, _, first, last) in enumerate(phases):
        wait_all(src, send_sem.at[p], first, last)
    for store in stores:
        store.wait()


def copy_out(*refs):
    sources, targets, held, sem = refs[:4], refs[4:8], refs[8:12], refs[12]
    steps = []
    for i, (source, between, target) in enumerate(zip(sources, held, targets, strict=True)):
        fetch = pltpu.make_async_copy(source, between, sem.at[0, i])
        fetch.start()
        steps.append((fetch, pltpu.make_async_copy(between, target, sem.at[1, i])))
    for fetch, store in steps:
        fetch.wait()
        store.start()
    for _, store in steps:
        store.wait()


def on_device(queries, keys, values, layer_grad, out_proj, cluster, slot, tile_of):
    tokens, heads, size = queries.shape
    n_seq, n_head = lax.axis_size("seq"), lax.axis_size("head")
    rows = n_seq * CAP
    flat = (tokens, heads * size)
    out_proj = out_proj.reshape(heads * size, -1)
    arguments = (queries, keys, values, layer_grad, out_proj, cluster, slot, tile_of)
    shapes = [jax.ShapeDtypeStruct((tokens, heads, size), BF16)] * 3
    shapes.append(jax.ShapeDtypeStruct((heads, 8, size), F32))
    results = pl.pallas_call(
        functools.partial(kernel, n_seq, n_head),
        out_shape=shapes,
        in_specs=[pl.BlockSpec(memory_space=pl.ANY)] * 8,
        out_specs=[pl.BlockSpec(memory_space=pl.ANY)] * 4,
        scratch_shapes=[pltpu.VMEM(a.shape, a.dtype) for a in (*arguments, *shapes)]
        + [
            pltpu.VMEM((n_head,) + layer_grad.shape, BF16),
            pltpu.VMEM(flat, BF16),
            pltpu.VMEM((heads, rows, tokens), BF16),
            pltpu.VMEM((heads, tokens, rows), BF16),
            pltpu.VMEM((heads, n_seq, CAP, 4 * size), BF16),
            pltpu.VMEM((heads, n_seq, CAP, 4 * size), BF16),
            pltpu.VMEM((n_seq, 1, 128), F32),
            pltpu.VMEM((n_seq, 1, 128), F32),
            pltpu.VMEM((heads, n_seq, CAP, 3 * size), BF16),
            pltpu.VMEM((heads, n_seq, CAP, 3 * size), BF16),
            pltpu.VMEM((rows, size), F32),
            pltpu.VMEM((rows, size), F32),
            pltpu.VMEM((tokens, 3 * size), F32),
            pltpu.SemaphoreType.DMA,
            pltpu.SemaphoreType.DMA,
            pltpu.SemaphoreType.DMA,
            pltpu.SemaphoreType.DMA,
            pltpu.SemaphoreType.DMA((3 * heads + 1,)),
            pltpu.SemaphoreType.DMA((3 * heads + 1,)),
            pltpu.SemaphoreType.DMA((len(arguments),)),
            pltpu.SemaphoreType.DMA((len(shapes),)),
        ],
        compiler_params=pltpu.CompilerParams(
            collective_id=0, has_side_effects=True, vmem_limit_bytes=60 << 20
        ),
        name="routed_attention",
    )(*arguments)
    return pl.pallas_call(
        copy_out,
        out_shape=shapes,
        in_specs=[pl.BlockSpec(memory_space=pl.ANY)] * 4,
        out_specs=[pl.BlockSpec(memory_space=pl.ANY)] * 4,
        scratch_shapes=[pltpu.VMEM(a.shape, a.dtype) for a in shapes]
        + [pltpu.SemaphoreType.DMA((2, 4))],
        compiler_params=pltpu.CompilerParams(vmem_limit_bytes=60 << 20),
        name="copy_out",
    )(*results)

def solution(mesh):
    in_specs = (
        P("seq", "head", None),
        P("seq", "head", None),
        P("seq", "head", None),
        P("seq", "head"),
        P("head", None, None),
        P("head", "seq"),
        P("head", "seq"),
        P("head", None),
    )
    out_specs = (
        P("seq", "head", None),
        P("seq", "head", None),
        P("seq", "head", None),
        P("head", "seq", None),
    )
    return jax.shard_map(
        on_device, mesh=mesh, in_specs=in_specs, out_specs=out_specs, check_vma=False
    )
```

```python
import functools

import jax
import jax.numpy as jnp
from jax import lax
from jax.experimental import pallas as pl
from jax.experimental.pallas import tpu as pltpu
from jax.sharding import PartitionSpec as P

MESH = pl.DeviceIdType.MESH
CAP = 16
Z = 16
F32 = jnp.float32
BF16 = jnp.bfloat16
UNUSED = 1 << 20


def iota(shape, dim):
    return lax.broadcasted_iota(jnp.int32, shape, dim)


def one_hot(mask):
    return jnp.where(mask, 1.0, 0.0).astype(BF16)


def matmul(a, b):
    return jnp.dot(a, b, preferred_element_type=F32)


def matmul_nt(a, b):
    return lax.dot_general(a, b, (((1,), (1,)), ((), ())), preferred_element_type=F32)


def matmul_tn(a, b):
    return lax.dot_general(a, b, (((0,), (0,)), ((), ())), preferred_element_type=F32)


def kernel(
    n_seq,
    n_head,
    *refs,
):
    inputs, outputs, held, results, refs = refs[:8], refs[8:12], refs[12:20], refs[20:24], refs[24:]
    query_grad, key_grad, value_grad, centroid = results
    queries, keys, values, layer_grad, out_proj, cluster, slot, tile_of = held
    (
        gathered,
        grads_out,
        pack,
        unpack,
        rows_send,
        rows_recv,
        meta_send,
        meta_recv,
        ret_send,
        ret_recv,
        key_sum,
        value_sum,
        grads_back,
        gather_send_sem,
        gather_recv_sem,
        meta_send_sem,
        meta_recv_sem,
        send_sem,
        recv_sem,
        held_sem,
        result_sem,
    ) = refs
    me = lax.axis_index("seq")
    my_head = lax.axis_index("head")
    me_y, me_z = me // Z, me % Z
    n_y = n_seq // Z
    heads, tokens = cluster.shape
    clusters = tile_of.shape[1]
    size = queries.shape[2]
    rows = n_seq * CAP
    columns = layer_grad.shape[1]
    others = n_seq - 1

    def ahead(k):
        return {"seq": lax.rem(me_y + k // Z, n_y) * Z + lax.rem(me_z + k % Z, Z)}

    def behind(k):
        return {"seq": lax.rem(me_y + n_y - k // Z, n_y) * Z + lax.rem(me_z + Z - k % Z, Z)}

    def peer(j):
        return {"head": lax.rem(my_head + j, n_head)}

    fetches = [
        pltpu.make_async_copy(source, target, held_sem.at[i])
        for i, (source, target) in enumerate(zip(inputs, held, strict=True))
    ]
    for fetch in fetches[::-1]:
        fetch.start()

    barrier = pltpu.get_barrier_semaphore()

    @pl.loop(1, n_seq)
    def _(k):
        pl.semaphore_signal(barrier, inc=1, device_id=ahead(k), device_id_type=MESH)

    @pl.loop(1, n_head)
    def _(j):
        pl.semaphore_signal(barrier, inc=1, device_id=peer(j), device_id_type=MESH)

    def remote(src, dst, sent, received, target):
        return pltpu.make_async_remote_copy(
            src_ref=src,
            dst_ref=dst,
            send_sem=sent,
            recv_sem=received,
            device_id=target,
            device_id_type=MESH,
        )

    def wait_all(buffer, sem, first, last):
        part = buffer.at[pl.ds(first, last - first)]
        pltpu.make_async_copy(part, part, sem).wait()

    def lanes(ref, h, first, count):
        return ref.at[h, :, :, pl.ds(first * size, count * size)]

    phases = [
        (lanes(rows_send, 0, 0, 3), lanes(rows_recv, 0, 0, 3), ahead, 1, n_seq),
        (lanes(rows_send, 0, 3, 1), lanes(rows_recv, 0, 3, 1), ahead, 1, n_seq),
    ]
    phases += [(rows_send.at[h], rows_recv.at[h], ahead, 1, n_seq) for h in range(1, heads)]
    phases += [
        (ret_send.at[h], ret_recv.at[h], behind, max(1, first), first + n_seq // 2)
        for h in range(heads)
        for first in (0, n_seq // 2)
    ]

    def nth(i):
        return i

    def message(p, i):
        src, dst, target, _, _ = phases[p]
        k = nth(i)
        return remote(src.at[k], dst.at[k], send_sem.at[p], recv_sem.at[p], target(k))

    def issue(p, first=None, last=None):
        @pl.loop(first or phases[p][3], last or phases[p][4])
        def _(i):
            message(p, i).start()

    def arrived(p):
        _, dst, _, first, last = phases[p]
        wait_all(dst, recv_sem.at[p], first, last)

    places = []

    def route(h):
        ids = cluster[pl.ds(h, 1), :]
        table = jnp.broadcast_to(tile_of[pl.ds(h, 1), :], (8, clusters))
        table = jnp.where(iota((8, clusters), 0) == 0, table >> 3, table & 7)
        chosen = one_hot(iota((clusters, tokens), 0) == ids)
        found = matmul(table.astype(F32).astype(BF16), chosen).astype(jnp.int32)
        owner, local = found[0:1], found[1:2]
        block = (((owner >> 4) - me_y + n_y) & (n_y - 1)) * Z + (((owner & 15) - me_z + Z) & (Z - 1))
        in_block = iota((n_seq, tokens), 0) == block
        earlier = one_hot(iota((tokens, tokens), 0) < iota((tokens, tokens), 1))
        before = matmul(one_hot(in_block), earlier)
        place = jnp.sum(jnp.where(in_block, before, 0.0), axis=0, keepdims=True)
        place_int = place.astype(jnp.int32)
        target = block * CAP + place_int
        places.append((block, place, local, target))

    def labels():
        meta = jnp.zeros((n_seq, 128), F32)
        for h, (block, place, local, _) in enumerate(places):
            in_block = iota((n_seq, tokens), 0) == block
            label = (local * 4 + slot[pl.ds(h, 1), :] + 1).astype(F32)
            at = iota((128, tokens), 0) == place.astype(jnp.int32) + CAP * h
            meta += matmul_nt(one_hot(in_block), jnp.where(at, label, 0.0).astype(BF16))
        meta_send[...] = meta.reshape(n_seq, 1, 128)

        @pl.loop(1, n_seq)
        def _(k):
            remote(
                meta_send.at[k], meta_recv.at[k], meta_send_sem, meta_recv_sem, ahead(k)
            ).start()

        meta_recv[0] = meta_send[0]

    def route_back(h):
        block, place, _, _ = places[h]
        same = one_hot(iota((tokens, tokens), 0) == iota((tokens, tokens), 1))
        both = jnp.where(
            iota((8, tokens), 0) == 0, block.astype(F32), jnp.broadcast_to(place, (8, tokens))
        ).astype(BF16)
        both = matmul_nt(same, both).astype(jnp.int32)
        unpack[h] = one_hot(iota((tokens, rows), 1) == both[:, 0:1] * CAP + both[:, 1:2])

    def of_head(ref):
        return lambda h: ref[:, h, :]

    token_rows = [of_head(ref) for ref in (queries, keys, values)]

    def grads_of(h):
        return grads_out[:, pl.ds(h * size, size)]

    step = 256

    def pack_step(h, first, first_lane, cuts):
        part = pack[h, pl.ds(first, step), :]
        for i, source in enumerate(cuts):
            moved = matmul(part, source).astype(BF16).reshape(step // CAP, CAP, size)
            blocks = pl.ds(first // CAP, step // CAP)
            rows_send[h, blocks, :, pl.ds((first_lane + i) * size, size)] = moved

    def pack_part(h, first_lane, cuts):
        cuts = [cut(h) for cut in cuts]
        for first in range(0, rows, step):
            pack_step(h, first, first_lane, cuts)

    def select(h, first):
        at = iota((step, tokens), 0) + first
        pack[h, pl.ds(first, step), :] = one_hot(at == places[h][3])

    for fetch in fetches[5:]:
        fetch.wait()
    route(0)
    for fetch in fetches[:5]:
        fetch.wait()
    cuts = [cut(0) for cut in token_rows]
    for first in range(0, rows, step):
        select(0, first)
        pack_step(0, first, 0, cuts)
        if first == 0:
            pl.semaphore_wait(barrier, others + n_head - 1)
        issue(0, max(1, first // CAP), (first + step) // CAP)
        if first == 0:

            @pl.loop(1, n_head)
            def _(j):
                remote(
                    layer_grad, gathered.at[j], gather_send_sem, gather_recv_sem, peer(j)
                ).start()

    for h in range(1, heads):
        route(h)
        for first in range(0, rows, step):
            select(h, first)
    labels()
    for h in range(1, heads):
        pack_part(h, 0, token_rows)

    wait_all(gathered, gather_recv_sem, 1, n_head)
    total = jnp.zeros((tokens, heads * size), F32)
    for j in range(n_head):
        part = layer_grad[...] if j == 0 else gathered[j]
        source = lax.rem(my_head + n_head - j, n_head)
        weight = out_proj[:, pl.ds(pl.multiple_of(source * columns, columns), columns)]
        total += matmul_nt(part, weight)
    grads_out[...] = total.astype(BF16)
    pack_part(0, 3, (grads_of,))
    issue(1)
    for h in range(1, heads):
        pack_part(h, 3, (grads_of,))
    issue(2)
    for h in range(heads):
        rows_recv[h, 0] = rows_send[h, 0]

    def codes(index, label):
        k = index >> 4
        source = ((me_y - (k >> 4) + n_y) & (n_y - 1)) * Z + ((me_z - (k & 15) + Z) & (Z - 1))
        used = label > 0
        tile = (label - 1) >> 2
        code = tile * 256 + source * 3 + ((label - 1) & 3)
        return used, tile, code

    factor = size ** (-0.5)
    block_rows = 256
    turns = rows // block_rows

    def tiles(h):
        received = meta_recv[...].reshape(n_seq, 128).astype(BF16)
        lane_of = one_hot(iota((128, rows), 0) == (iota((128, rows), 1) & 15) + CAP * h)
        spread = matmul(received, lane_of)
        own = iota((n_seq, rows), 0) == iota((n_seq, rows), 1) >> 4
        label_row = jnp.sum(jnp.where(own, spread, 0.0), axis=0, keepdims=True).astype(jnp.int32)
        used_row, tile_row, code_row = codes(iota((1, rows), 1), label_row)
        code_row = jnp.where(used_row, code_row, 2 * UNUSED)
        member = one_hot((iota((8, rows), 0) == tile_row) & used_row)
        key_sum[...] = jnp.zeros_like(key_sum)
        value_sum[...] = jnp.zeros_like(value_sum)
        every_key = rows_recv[h, :, :, pl.ds(size, size)].reshape(rows, size)
        every_value = rows_recv[h, :, :, pl.ds(2 * size, size)].reshape(rows, size)

        @pl.loop(0, turns)
        def _(b):
            start = pl.multiple_of(b * (block_rows // CAP), block_rows // CAP)
            chunk = pl.ds(start, block_rows // CAP)
            index = iota((block_rows, n_seq), 0) + b * block_rows
            picked = matmul(one_hot(iota((block_rows, n_seq), 1) == index >> 4), received)
            index = iota((block_rows, 128), 0) + b * block_rows
            lane = iota((block_rows, 128), 1) == (index & 15) + CAP * h
            label = jnp.sum(jnp.where(lane, picked, 0.0), axis=1, keepdims=True).astype(jnp.int32)
            used, tile, code = codes(iota((block_rows, 1), 0) + b * block_rows, label)
            low = jnp.where(used, tile * 256, UNUSED)
            code = jnp.where(used, code, -1)
            query = rows_recv[h, chunk, :, pl.ds(0, size)].reshape(block_rows, size)
            grad = rows_recv[h, chunk, :, pl.ds(3 * size, size)].reshape(block_rows, size)
            scores = matmul_nt(query, every_key) * factor
            allowed = (code_row >= low) & (code_row <= code)
            largest = jnp.max(jnp.where(allowed, scores, -1e30), axis=1, keepdims=True)
            weights = jnp.where(allowed, jnp.exp(scores - largest), 0.0)
            whole = jnp.sum(weights, axis=1, keepdims=True)
            probs = weights / jnp.where(used, whole, 1.0)
            probs_low = probs.astype(BF16)
            dprobs = matmul_nt(grad, every_value)
            stat = jnp.sum(probs_low.astype(F32) * dprobs, axis=1, keepdims=True)
            dscores = (probs * (dprobs - stat)).astype(BF16)
            ret_send[h, chunk, :, pl.ds(0, size)] = (
                (matmul(dscores, every_key) * factor)
                .astype(BF16)
                .reshape(block_rows // CAP, CAP, size)
            )
            key_sum[...] += matmul_tn(dscores, query)
            value_sum[...] += matmul_tn(probs_low, grad)

        ret_send[h, :, :, pl.ds(size, size)] = (
            (key_sum[...] * factor).astype(BF16).reshape(n_seq, CAP, size)
        )
        ret_send[h, :, :, pl.ds(2 * size, size)] = (
            value_sum[...].astype(BF16).reshape(n_seq, CAP, size)
        )
        ret_recv[h, 0] = ret_send[h, 0]
        return member

    def centroids(h, member):
        unit = jnp.zeros((rows, size), F32)
        for i in range(2):
            wide = rows_recv[h, :, :, pl.ds(i * size, size)].reshape(rows, size).astype(F32)
            unit += wide * lax.rsqrt(jnp.sum(wide * wide, axis=1, keepdims=True) + 1e-06)
        high = unit.astype(BF16)
        rest = (unit - high.astype(F32)).astype(BF16)
        centroid[h] = matmul(member, high) + matmul(member, rest)

    stores = [
        pltpu.make_async_copy(source, target, result_sem.at[i])
        for i, (source, target) in enumerate(zip(results, outputs, strict=True))
    ]

    def finish(h, p):
        part = n_seq // 2
        for first in (0, part):
            arrived(p + first // part)
            blocks, columns = pl.ds(first, part), pl.ds(first * CAP, part * CAP)
            returned = ret_recv[h, blocks].reshape(part * CAP, 3 * size)
            moved = matmul(unpack[h, :, columns], returned)
            if first == 0:
                grads_back[...] = moved
            else:
                moved += grads_back[...]
        for i, grad_ref in enumerate((query_grad, key_grad, value_grad)):
            grad_ref[:, h, :] = moved[:, i * size : (i + 1) * size].astype(BF16)
            if h == heads - 1:
                stores[i].start()

    wait_all(meta_recv, meta_recv_sem, 1, n_seq)
    arrived(0)
    arrived(1)
    member = tiles(0)
    issue(3)
    issue(4)
    centroids(0, member)
    route_back(0)
    arrived(2)
    member = tiles(1)
    issue(5)
    issue(6)
    centroids(1, member)
    route_back(1)
    stores[3].start()
    finish(0, 3)
    finish(1, 5)

    wait_all(gathered, gather_send_sem, 1, n_head)
    wait_all(meta_send, meta_send_sem, 1, n_seq)
    for p, (src, _, _, first, last) in enumerate(phases):
        wait_all(src, send_sem.at[p], first, last)
    for store in stores:
        store.wait()


def copy_out(*refs):
    sources, targets, held, sem = refs[:4], refs[4:8], refs[8:12], refs[12]
    steps = []
    for i, (source, between, target) in enumerate(zip(sources, held, targets, strict=True)):
        fetch = pltpu.make_async_copy(source, between, sem.at[0, i])
        fetch.start()
        steps.append((fetch, pltpu.make_async_copy(between, target, sem.at[1, i])))
    for fetch, store in steps:
        fetch.wait()
        store.start()
    for _, store in steps:
        store.wait()


def on_device(queries, keys, values, layer_grad, out_proj, cluster, slot, tile_of):
    tokens, heads, size = queries.shape
    n_seq, n_head = lax.axis_size("seq"), lax.axis_size("head")
    rows = n_seq * CAP
    flat = (tokens, heads * size)
    out_proj = out_proj.reshape(heads * size, -1)
    arguments = (queries, keys, values, layer_grad, out_proj, cluster, slot, tile_of)
    shapes = [jax.ShapeDtypeStruct((tokens, heads, size), BF16)] * 3
    shapes.append(jax.ShapeDtypeStruct((heads, 8, size), F32))
    results = pl.pallas_call(
        functools.partial(kernel, n_seq, n_head),
        out_shape=shapes,
        in_specs=[pl.BlockSpec(memory_space=pl.ANY)] * 8,
        out_specs=[pl.BlockSpec(memory_space=pl.ANY)] * 4,
        scratch_shapes=[pltpu.VMEM(a.shape, a.dtype) for a in (*arguments, *shapes)]
        + [
            pltpu.VMEM((n_head,) + layer_grad.shape, BF16),
            pltpu.VMEM(flat, BF16),
            pltpu.VMEM((heads, rows, tokens), BF16),
            pltpu.VMEM((heads, tokens, rows), BF16),
            pltpu.VMEM((heads, n_seq, CAP, 4 * size), BF16),
            pltpu.VMEM((heads, n_seq, CAP, 4 * size), BF16),
            pltpu.VMEM((n_seq, 1, 128), F32),
            pltpu.VMEM((n_seq, 1, 128), F32),
            pltpu.VMEM((heads, n_seq, CAP, 3 * size), BF16),
            pltpu.VMEM((heads, n_seq, CAP, 3 * size), BF16),
            pltpu.VMEM((rows, size), F32),
            pltpu.VMEM((rows, size), F32),
            pltpu.VMEM((tokens, 3 * size), F32),
            pltpu.SemaphoreType.DMA,
            pltpu.SemaphoreType.DMA,
            pltpu.SemaphoreType.DMA,
            pltpu.SemaphoreType.DMA,
            pltpu.SemaphoreType.DMA((3 * heads + 1,)),
            pltpu.SemaphoreType.DMA((3 * heads + 1,)),
            pltpu.SemaphoreType.DMA((len(arguments),)),
            pltpu.SemaphoreType.DMA((len(shapes),)),
        ],
        compiler_params=pltpu.CompilerParams(
            collective_id=0, has_side_effects=True, vmem_limit_bytes=60 << 20
        ),
        name="routed_attention",
    )(*arguments)
    return pl.pallas_call(
        copy_out,
        out_shape=shapes,
        in_specs=[pl.BlockSpec(memory_space=pl.ANY)] * 4,
        out_specs=[pl.BlockSpec(memory_space=pl.ANY)] * 4,
        scratch_shapes=[pltpu.VMEM(a.shape, a.dtype) for a in shapes]
        + [pltpu.SemaphoreType.DMA((2, 4))],
        compiler_params=pltpu.CompilerParams(vmem_limit_bytes=60 << 20),
        name="copy_out",
    )(*results)

def solution(mesh):
    in_specs = (
        P("seq", "head", None),
        P("seq", "head", None),
        P("seq", "head", None),
        P("seq", "head"),
        P("head", None, None),
        P("head", "seq"),
        P("head", "seq"),
        P("head", None),
    )
    out_specs = (
        P("seq", "head", None),
        P("seq", "head", None),
        P("seq", "head", None),
        P("head", "seq", None),
    )
    return jax.shard_map(
        on_device, mesh=mesh, in_specs=in_specs, out_specs=out_specs, check_vma=False
    )
```
